512 devices in a mesh: gx: 128 (over z, y, core), gy: 4 (over x).
Axes of the slice: x: 4, y: 4, z: 16, core: 2. Of those that a mesh axis runs over, the one named last changes fastest.
Arguments:
- x_data: float32 [256, 256, 256, 16], P('gx', None, 'gy'), as said below
- start_x: float32 [256, 64], replicated, may hold values from -6 to 6
- start_y: float32 [256, 64], replicated, may hold values from -6 to 6
- start_z: float32 [256, 64], replicated, may hold values from -6 to 6
Outputs:
- core: float32 [1024, 64, 64], P('gx', 'gy')
- factor_x: float32 [256, 64], replicated
- factor_y: float32 [256, 64], replicated
- factor_z: float32 [256, 64], replicated
The draws below stay inside these ranges and needn't reach their ends.
Inputs may be any that keep to these rules, and one draw needn't show every extreme that they name: `x_data`: real-valued field samples.
All inputs are finite; a program needn't handle non-finite values.
Results may differ from the reference program's by a relative error of at most 0.0003.
Values sent between devices are 32-bit elements; how exact they have to be, the bound alone decides.
A program may use at most 64 MiB of HBM per device.

```python
import jax
import jax.numpy as jnp
from jax import lax

NX = 256
NY = 256
NZ = 256
S = 16
RANK = 64
ITERS = 4


def draw_x_data(key, part):
    key = jax.random.fold_in(key, 11)
    keys = jax.random.split(key, 7)
    noise = jax.random.truncated_normal(keys[0], -4.0, 4.0, (NX, NZ, NY, S), jnp.float32)
    amplitude = 0.12
    along_x = jax.random.truncated_normal(keys[1], -3.0, 3.0, (6, NX), jnp.float32)
    along_z = jax.random.truncated_normal(keys[2], -3.0, 3.0, (6, NZ), jnp.float32)
    along_y = jax.random.truncated_normal(keys[3], -3.0, 3.0, (6, NY), jnp.float32)
    along_s = jax.random.truncated_normal(keys[4], -3.0, 3.0, (6, S), jnp.float32)
    structured = jnp.zeros((NX, NZ, NY, S), jnp.float32)
    for term in range(6):
        structured = structured + along_x[term][:, None, None, None] * along_z[term][None, :, None, None] * along_y[term][None, None, :, None] * along_s[term][None, None, None, :]
    species = jnp.exp(jax.random.uniform(keys[5], (S,), jnp.float32, -1.204, 1.0986))
    ramp = 1.0 + 2.0 * jnp.arange(NZ, dtype=jnp.float32) / (NZ - 1)
    zscale = ramp * jax.random.uniform(keys[6], (NZ,), jnp.float32, 0.7, 1.4)
    field = (noise + amplitude * structured) * species[None, None, None, :] * zscale[None, :, None, None]
    return field.astype(jnp.float32)


def bell_draw(own_key, shape, scale, most, held_as=jnp.bfloat16):
    entries = jax.random.normal(own_key, shape, jnp.float32) * scale
    return jnp.minimum(jnp.maximum(entries, -most), most).astype(held_as)


def setup_inputs(seed: int = 0) -> dict:
    key_of = jax.random.split(jax.random.key(seed), 5)
    x_data = draw_x_data(jax.random.fold_in(key_of[4], 71), 0)
    start_x = bell_draw(key_of[1], (NX, RANK), 1.0, 6.0, jnp.float32)
    start_y = bell_draw(key_of[2], (NY, RANK), 1.0, 6.0, jnp.float32)
    start_z = bell_draw(key_of[3], (NZ, RANK), 1.0, 6.0, jnp.float32)
    return dict(x_data=x_data, start_x=start_x, start_y=start_y, start_z=start_z)


def iterate_factor(gram, start):
    block = start
    for step in range(ITERS):
        image = jnp.dot(gram, block, precision=lax.Precision.HIGHEST)
        inner = jnp.dot(image.T, image, precision=lax.Precision.HIGHEST)
        lower = jnp.linalg.cholesky(inner)
        block = jax.scipy.linalg.solve_triangular(lower, image.T, lower=True).T
    return block

def reference(x_data, start_x, start_y, start_z):
    high = lax.Precision.HIGHEST
    gram_x = jnp.einsum('azys,bzys->ab', x_data, x_data, precision=high)
    factor_x = iterate_factor(gram_x, start_x)
    first_core = jnp.einsum('xk,xzys->kzys', factor_x, x_data, precision=high)
    gram_y = jnp.einsum('kzas,kzbs->ab', first_core, first_core, precision=high)
    factor_y = iterate_factor(gram_y, start_y)
    second_core = jnp.einsum('yl,kzys->kzls', factor_y, first_core, precision=high)
    gram_z = jnp.einsum('kals,kbls->ab', second_core, second_core, precision=high)
    factor_z = iterate_factor(gram_z, start_z)
    core = jnp.einsum('zm,kzls->lskm', factor_z, second_core, precision=high)
    core = core.reshape(RANK * S, RANK, RANK)
    return (core, factor_x, factor_y, factor_z)
```

```python
import functools

import jax
import jax.numpy as jnp
from jax import lax
from jax.experimental import pallas as pl
from jax.experimental.pallas import tpu as pltpu
from jax.sharding import PartitionSpec as P

ITERS = 4
MESH = pl.DeviceIdType.MESH
HIGHEST = lax.Precision.HIGHEST
Z_STEPS = [8] + [sign * d for d in range(7, 0, -1) for sign in (1, -1)]


def dot(a, b, ca, cb):
    return lax.dot_general(
        a, b, (((ca,), (cb,)), ((), ())), precision=HIGHEST, preferred_element_type=jnp.float32
    )


def position():
    g = lax.axis_index("gx")
    return lax.axis_index("gy"), (g // 2) % 4, g // 8, g % 2


def device(x, y, z, c):
    return ((z * 4 + y) * 2 + c, x)


def plane_index(x, y, c):
    return (y * 2 + c) * 4 + x


def plane_peer(i, x, y, c):
    return (x + i % 4) % 4, (y + i // 8) % 4, (c + (i // 4) % 2) % 2


def inverse_cholesky(p):
    n = 64
    row = lax.broadcasted_iota(jnp.int32, (n, n), 0)
    col = lax.broadcasted_iota(jnp.int32, (n, n), 1)
    m = jnp.concatenate([p, (row == col).astype(jnp.float32)], axis=1)
    sub = lax.broadcasted_iota(jnp.int32, (8, 128), 0)
    blocks = [m[8 * i : 8 * i + 8, :] for i in range(8)]
    out = []
    for k in range(8):
        cols = {
            (i, j): jnp.broadcast_to(blocks[i][:, 8 * k + j : 8 * k + j + 1], (8, 128))
            for j in range(8)
            for i in range(k, 8)
        }
        rows = [jnp.broadcast_to(blocks[k][j : j + 1, :], (8, 128)) for j in range(8)]
        splat = {
            (r, j): jnp.broadcast_to(cols[k, j][r : r + 1, :], (8, 128))
            for j in range(8)
            for r in range(j, 8)
        }
        for j in range(8):
            scale = lax.rsqrt(splat[j, j])
            for r in range(j + 1, 8):
                splat[r, j] = splat[r, j] * scale
            for i in range(k + 1, 8):
                cols[i, j] = cols[i, j] * scale
            rows[j] = rows[j] * scale
            for t in range(j + 1, 8):
                for r in range(t, 8):
                    splat[r, t] = splat[r, t] - splat[r, j] * splat[t, j]
                for i in range(k + 1, 8):
                    cols[i, t] = cols[i, t] - cols[i, j] * splat[t, j]
                rows[t] = rows[t] - rows[j] * splat[t, j]
        for i in range(k + 1, 8):
            for j in range(8):
                blocks[i] = blocks[i] - cols[i, j] * rows[j]
        done = rows[0]
        for j in range(1, 8):
            done = jnp.where(sub == j, rows[j], done)
        out.append(done)
    return jnp.concatenate(out, axis=0)[:, n:]


def factor(gram, start_t, out_ref):
    out_ref[...] = start_t

    def step(_, carry):
        image = dot(out_ref[...], gram[...], 1, 0)
        inner = dot(image, image, 1, 1)
        out_ref[...] = dot(inverse_cholesky(inner), image, 1, 0)
        return carry

    lax.fori_loop(0, ITERS, step, 0)


def permutation(kind):
    old = lax.broadcasted_iota(jnp.int32, (256, 256), 0)
    new = lax.broadcasted_iota(jnp.int32, (256, 256), 1)
    if kind == "x":
        source = (new % 128) * 2 + new // 128
    else:
        source = (new % 32) * 8 + new // 32
    return (old == source).astype(jnp.float32)


def swap_blocks(parts):
    lane = lax.broadcasted_iota(jnp.int32, (32, 128), 1) // 16
    parts = list(parts)
    for bit in (1, 2, 4):
        high = (lane & bit) != 0
        new = list(parts)
        for a in range(8):
            if a & bit == 0:
                lo, hi = parts[a], parts[a + bit]
                new[a] = jnp.where(high, pltpu.roll(hi, 16 * bit, 1), lo)
                new[a + bit] = jnp.where(high, hi, pltpu.roll(lo, 128 - 16 * bit, 1))
        parts = new
    return parts


def all_reduce(gram, r1, r2, part, out, sems):
    x, y, z, c = position()
    own = plane_index(x, y, c)

    def send_rows(i, carry):
        tx, ty, tc = plane_peer(i, x, y, c)
        rows = pl.ds(pl.multiple_of(plane_index(tx, ty, tc) * 8, 8), 8)
        pltpu.make_async_remote_copy(
            gram.at[rows, :], r1.at[i], sems.at[0], sems.at[1],
            device_id=device(tx, ty, z, tc), device_id_type=MESH,
        ).start()
        return carry

    for i in range(1, 32):
        send_rows(i, 0)
    mine = pl.ds(pl.multiple_of(own * 8, 8), 8)
    total = gram[mine, :]
    others = r1.at[pl.ds(1, 31)]
    pltpu.make_async_copy(others, others, sems.at[1]).wait()
    for i in range(1, 32):
        total = total + r1[i]
    part[0] = total
    r2[z] = total
    for dz in Z_STEPS:
        pltpu.make_async_remote_copy(
            part.at[0], r2.at[z], sems.at[2], sems.at[3],
            device_id=device(x, y, (z + dz + 16) % 16, c), device_id_type=MESH,
        ).start()
    fifteen = r1.at[pl.ds(1, 15)]
    pltpu.make_async_copy(fifteen, fifteen, sems.at[3]).wait()
    total = r2[0]
    for i in range(1, 16):
        total = total + r2[i]
    part[1] = total
    out[mine, :] = total
    for i in range(1, 32):
        tx, ty, tc = plane_peer(i, x, y, c)
        pltpu.make_async_remote_copy(
            part.at[1], out.at[mine, :], sems.at[4], sems.at[5],
            device_id=device(tx, ty, z, tc), device_id_type=MESH,
        ).start()
    pltpu.make_async_copy(others, others, sems.at[5]).wait()
    pltpu.make_async_copy(others, others, sems.at[0]).wait()
    pltpu.make_async_copy(fifteen, fifteen, sems.at[2]).wait()
    pltpu.make_async_copy(others, others, sems.at[4]).wait()


def kernel(
    xt, sx, sy, sz, core, fx, fy, fz,
    outgoing, by_z, lines, matrix, fc, sc, q, d, at, perm_x, perm_z, vt, halves, gram, total, r1, r2, part,
    ar_sems, z_recv, sems,
):
    x, y, z, c = position()
    own = plane_index(x, y, c)
    barrier = pltpu.get_barrier_semaphore()
    for i in range(1, 32):
        tx, ty, tc = plane_peer(i, x, y, c)
        pl.semaphore_signal(barrier, 1, device_id=device(tx, ty, z, tc), device_id_type=MESH)
    for dz in range(1, 16):
        for dc in range(2):
            pl.semaphore_signal(
                barrier, 1, device_id=device(x, y, (z + dz) % 16, (c + dc) % 2), device_id_type=MESH
            )

    sub = lax.broadcasted_iota(jnp.int32, (8, 128), 0)
    lane = lax.broadcasted_iota(jnp.int32, (8, 128), 1)
    keep = (sub < 4) == (lane < 64)

    def turn(half, carry):
        for s in range(16):
            t = xt[:, s, pl.ds(pl.multiple_of(half * 128, 128), 128)].T
            for zb in range(16):
                tile = t[zb * 8 : zb * 8 + 8, :]
                moved = pltpu.roll(pltpu.roll(tile, 4, 0), 64, 1)
                outgoing[s, half * 16 + zb] = jnp.where(keep, tile, moved)
        return carry

    lax.fori_loop(0, 2, turn, 0)
    perm_x[...] = permutation("x")
    perm_z[...] = permutation("z")
    vt[0] = dot(sx[...], perm_x[...], 1, 0)
    vt[1] = dot(sz[...], perm_z[...], 1, 0)

    pl.semaphore_wait(barrier, 61)

    for k, dz in enumerate(Z_STEPS):
        tz = (z + dz + 16) % 16
        pltpu.make_async_remote_copy(
            outgoing.at[tz], by_z.at[z], sems.at[0], z_recv.at[k],
            device_id=device(x, y, tz, c), device_id_type=MESH,
        ).start()

    yc = y * 2 + c

    def forward(buffer, zs, slot):
        def one(i, carry):
            tx, ty, tc = plane_peer(i, x, y, c)
            pltpu.make_async_remote_copy(
                buffer.at[slot, plane_index(tx, ty, tc)], lines.at[x, zs * 8 + yc],
                sems.at[1], sems.at[2],
                device_id=device(tx, ty, z, tc), device_id_type=MESH,
            ).start()
            return carry

        lax.fori_loop(1, 32, one, 0)
        lines[x, zs * 8 + yc] = buffer[slot, own]

    forward(outgoing, z, z)
    for k, dz in enumerate(Z_STEPS):
        arrived = by_z.at[0]
        pltpu.make_async_copy(arrived, arrived, z_recv.at[k]).wait()
        zs = (z - dz + 16) % 16
        forward(by_z, zs, zs)
    most = outgoing.at[pl.ds(0, 15)]
    pltpu.make_async_copy(most, most, sems.at[0]).wait()
    tiles = outgoing.at[:, pl.ds(0, 31)]
    pltpu.make_async_copy(tiles, tiles, sems.at[2]).wait()
    pltpu.make_async_copy(tiles, tiles, sems.at[1]).wait()

    for cx in range(4):
        for zh in range(4):
            for p in range(2):
                matrix[p * 128 : p * 128 + 128, (cx * 4 + zh) * 128 : (cx * 4 + zh + 1) * 128] = (
                    lines[cx, :, p * 4 + zh, :]
                )
    gram[...] = dot(matrix[...], matrix[...], 1, 1)
    all_reduce(gram, r1.at[0], r2.at[0], part.at[0], total.at[0], ar_sems.at[0])
    factor(total.at[0], vt[0], vt.at[2])
    fx[...] = dot(vt[2], perm_x[...], 1, 1)

    low = lax.broadcasted_iota(jnp.int32, (64, 128), 1) < 64
    for zh in range(4):
        piece = [
            dot(vt[2], matrix[:, (cx * 4 + zh) * 128 : (cx * 4 + zh + 1) * 128], 1, 0)
            for cx in range(4)
        ]
        turned = [pltpu.roll(v, 64, 1) for v in piece]
        for pair in range(2):
            a, b = 2 * pair, 2 * pair + 1
            for zl, value in (
                (0, jnp.where(low, piece[a], turned[b])),
                (1, jnp.where(low, turned[a], piece[b])),
            ):
                zz = zl * 4 + zh
                for kb in range(4):
                    fc[kb * 128 + zz * 16 : kb * 128 + zz * 16 + 16, pair * 128 : pair * 128 + 128] = (
                        value[kb * 16 : kb * 16 + 16, :]
                    )
    gram[...] = dot(fc[...], fc[...], 0, 0)
    all_reduce(gram, r1.at[1], r2.at[1], part.at[1], total.at[1], ar_sems.at[1])
    factor(total.at[1], sy[...], fy)

    for lanes in range(2):
        halves[lanes] = fy[:, lanes * 128 : lanes * 128 + 128]
        for cy in range(4):
            for half in range(2):
                first = (cy * 2 + half) * 8
                vt[2, first : first + 8, lanes * 128 : lanes * 128 + 128] = halves[
                    lanes, pl.ds(32 * half + cy, 8, stride=4), :
                ]
    product = dot(vt[2], fc[...], 1, 1)
    for t in range(8):
        for cx in range(4):
            sc[t * 4 + cx] = product[t * 8 : t * 8 + 8, cx * 128 : cx * 128 + 128]

    for i in range(1, 32):
        tx, ty, tc = plane_peer(i, x, y, c)
        pltpu.make_async_remote_copy(
            sc.at[plane_index(tx, ty, tc)], q.at[own], sems.at[3], sems.at[4],
            device_id=device(tx, ty, z, tc), device_id_type=MESH,
        ).start()
    q[own] = sc[own]
    tiles = sc.at[pl.ds(0, 31)]
    pltpu.make_async_copy(tiles, tiles, sems.at[4]).wait()
    pltpu.make_async_copy(tiles, tiles, sems.at[3]).wait()

    for m in range(8):
        at[1, m * 32 : m * 32 + 32, :] = q[:, m, :]
    tc = z // 8
    for m in range(8):
        tz = c * 8 + m

        @pl.when(jnp.logical_or(tz != z, tc != c))
        def _():
            pltpu.make_async_remote_copy(
                at.at[1, pl.ds(m * 32, 32), :], d.at[z % 8], sems.at[5], sems.at[6],
                device_id=device(x, y, tz, tc), device_id_type=MESH,
            ).start()

        @pl.when(jnp.logical_and(tz == z, tc == c))
        def _():
            d[z % 8] = at[1, m * 32 : m * 32 + 32, :]

    lines_z = swap_blocks([at[1, m * 32 : m * 32 + 32, :] for m in range(8)])
    for zz in range(8):
        at[0, zz * 32 : zz * 32 + 32, :] = lines_z[zz]
    gram[...] = dot(at[0], at[0], 1, 1)
    all_reduce(gram, r1.at[2], r2.at[2], part.at[2], total.at[2], ar_sems.at[2])
    factor(total.at[2], vt[1], vt.at[2])
    fz[...] = dot(vt[2], perm_z[...], 1, 1)

    @pl.when(tc == c)
    def _():
        seven = d.at[pl.ds(0, 7)]
        pltpu.make_async_copy(seven, seven, sems.at[6]).wait()
        pltpu.make_async_copy(seven, seven, sems.at[5]).wait()

    @pl.when(tc != c)
    def _():
        pltpu.make_async_copy(d, d, sems.at[6]).wait()
        pltpu.make_async_copy(d, d, sems.at[5]).wait()

    by_zz = swap_blocks([d[s] for s in range(8)])
    for zz in range(8):
        at[0, zz * 32 : zz * 32 + 32, :] = by_zz[zz]
    result = dot(at[0], vt[2], 0, 1)
    for s in range(8):
        core[s] = result[s * 16 : s * 16 + 16, :]


def local(x_data, start_x, start_y, start_z):
    f32 = jnp.float32
    vmem = pl.BlockSpec(memory_space=pltpu.VMEM)
    xt = jnp.transpose(x_data, (0, 2, 3, 1)).reshape(128, 16, 256)
    core, fx, fy, fz = pl.pallas_call(
        kernel,
        out_shape=[
            jax.ShapeDtypeStruct((8, 16, 64), f32),
            jax.ShapeDtypeStruct((64, 256), f32),
            jax.ShapeDtypeStruct((64, 256), f32),
            jax.ShapeDtypeStruct((64, 256), f32),
        ],
        in_specs=[vmem] * 4,
        out_specs=[vmem] * 4,
        scratch_shapes=[
            pltpu.VMEM((16, 32, 8, 128), f32),
            pltpu.VMEM((16, 32, 8, 128), f32),
            pltpu.VMEM((4, 128, 8, 128), f32),
            pltpu.VMEM((256, 2048), f32),
            pltpu.VMEM((512, 256), f32),
            pltpu.VMEM((32, 8, 128), f32),
            pltpu.VMEM((32, 8, 128), f32),
            pltpu.VMEM((8, 32, 128), f32),
            pltpu.VMEM((2, 256, 128), f32),
            pltpu.VMEM((256, 256), f32),
            pltpu.VMEM((256, 256), f32),
            pltpu.VMEM((3, 64, 256), f32),
            pltpu.VMEM((2, 64, 128), f32),
            pltpu.VMEM((256, 256), f32),
            pltpu.VMEM((3, 256, 256), f32),
            pltpu.VMEM((3, 32, 8, 256), f32),
            pltpu.VMEM((3, 16, 8, 256), f32),
            pltpu.VMEM((3, 2, 8, 256), f32),
            pltpu.SemaphoreType.DMA((3, 6)),
            pltpu.SemaphoreType.DMA((15,)),
            pltpu.SemaphoreType.DMA((7,)),
        ],
        compiler_params=pltpu.CompilerParams(
            collective_id=0, has_side_effects=True, vmem_limit_bytes=40 << 20
        ),
    )(xt, start_x.T, start_y.T, start_z.T)
    return core, fx.T, fy.T, fz.T


def solution(mesh):
    placed = (P("gx", None, "gy", None), P(), P(), P())
    return jax.shard_map(
        local,
        mesh=mesh,
        in_specs=placed,
        out_specs=(P("gx", "gy", None), P(), P(), P()),
        check_vma=False,
    )
```

```python
import functools

import jax
import jax.numpy as jnp
from jax import lax
from jax.experimental import pallas as pl
from jax.experimental.pallas import tpu as pltpu
from jax.sharding import PartitionSpec as P

ITERS = 4
MESH = pl.DeviceIdType.MESH
HIGHEST = lax.Precision.HIGHEST
ROUNDS = 11
NEAR = (2, -2, 1, -1)
NEAR_AFTER = 4
Z_STEPS = [8] + [sign * d for d in range(7, 0, -1) for sign in (1, -1)]


def plane_distance(i):
    dx, dy, dc = i % 4, i // 8, (i // 4) % 2
    return min(dx, 4 - dx) + min(dy, 4 - dy) + dc


PLANE_STEPS = sorted(range(1, 32), key=lambda i: -plane_distance(i))


def dot(a, b, ca, cb):
    return lax.dot_general(
        a, b, (((ca,), (cb,)), ((), ())), precision=HIGHEST, preferred_element_type=jnp.float32
    )


def position():
    g = lax.axis_index("gx")
    return lax.axis_index("gy"), (g // 2) % 4, g // 8, g % 2


def device(x, y, z, c):
    return ((z * 4 + y) * 2 + c, x)


def plane_index(x, y, c):
    return (y * 2 + c) * 4 + x


def plane_peer(i, x, y, c):
    return (x + i % 4) % 4, (y + i // 8) % 4, (c + (i // 4) % 2) % 2


def inverse_cholesky(p):
    n = 64
    row = lax.broadcasted_iota(jnp.int32, (n, n), 0)
    col = lax.broadcasted_iota(jnp.int32, (n, n), 1)
    m = jnp.concatenate([p, (row == col).astype(jnp.float32)], axis=1)
    sub = lax.broadcasted_iota(jnp.int32, (8, 128), 0)
    blocks = [m[8 * i : 8 * i + 8, :] for i in range(8)]
    out = []
    for k in range(8):
        cols = {
            (i, j): jnp.broadcast_to(blocks[i][:, 8 * k + j : 8 * k + j + 1], (8, 128))
            for j in range(8)
            for i in range(k, 8)
        }
        rows = [jnp.broadcast_to(blocks[k][j : j + 1, :], (8, 128)) for j in range(8)]
        splat = {
            (r, j): jnp.broadcast_to(cols[k, j][r : r + 1, :], (8, 128))
            for j in range(8)
            for r in range(j, 8)
        }
        for j in range(8):
            scale = lax.rsqrt(splat[j, j])
            for r in range(j + 1, 8):
                splat[r, j] = splat[r, j] * scale
            for i in range(k + 1, 8):
                cols[i, j] = cols[i, j] * scale
            rows[j] = rows[j] * scale
            for t in range(j + 1, 8):
                for r in range(t, 8):
                    splat[r, t] = splat[r, t] - splat[r, j] * splat[t, j]
                for i in range(k + 1, 8):
                    cols[i, t] = cols[i, t] - cols[i, j] * splat[t, j]
                rows[t] = rows[t] - rows[j] * splat[t, j]
        for i in range(k + 1, 8):
            for j in range(8):
                blocks[i] = blocks[i] - cols[i, j] * rows[j]
        done = rows[0]
        for j in range(1, 8):
            done = jnp.where(sub == j, rows[j], done)
        out.append(done)
    return jnp.concatenate(out, axis=0)[:, n:]


def factor(gram, start_t):
    def step(_, block):
        image = dot(block, gram[...], 1, 0)
        return dot(inverse_cholesky(dot(image, image, 1, 1)), image, 1, 0)

    return lax.fori_loop(0, ITERS, step, start_t)


def permutation(kind):
    old = lax.broadcasted_iota(jnp.int32, (256, 256), 0)
    new = lax.broadcasted_iota(jnp.int32, (256, 256), 1)
    if kind == "x":
        source = (new % 128) * 2 + new // 128
    else:
        source = (new % 32) * 8 + new // 32
    return (old == source).astype(jnp.float32)


def swap_blocks(parts):
    lane = lax.broadcasted_iota(jnp.int32, (32, 128), 1) // 16
    parts = list(parts)
    for bit in (1, 2, 4):
        high = (lane & bit) != 0
        new = list(parts)
        for a in range(8):
            if a & bit == 0:
                lo, hi = parts[a], parts[a + bit]
                new[a] = jnp.where(high, pltpu.roll(hi, 16 * bit, 1), lo)
                new[a + bit] = jnp.where(high, hi, pltpu.roll(lo, 128 - 16 * bit, 1))
        parts = new
    return parts


def nothing():
    pass


def all_reduce(g, gram, pieces, r1, r2, part, full, sems, first=nothing, last=nothing):
    x, y, z, c = position()
    own = plane_index(x, y, c)
    row = lax.broadcasted_iota(jnp.int32, (128, 128), 0)
    col = lax.broadcasted_iota(jnp.int32, (128, 128), 1)
    low_right = g[128:, 128:]
    diagonal = jnp.sum(jnp.where(row == col, low_right, 0.0), axis=0, keepdims=True)
    t = jnp.where(row >= col, g[:128, :128], low_right)
    b = g[:128, 128:]
    beside = jnp.broadcast_to(diagonal, (8, 128))
    for q in range(16):
        pieces[q, 0:8] = b[8 * q : 8 * q + 8, :]
        pieces[16 + q, 0:8] = t[8 * q : 8 * q + 8, :]
        pieces[q, 8:16] = beside
        pieces[16 + q, 8:16] = beside
    nine = pl.ds(0, 9)
    for i in PLANE_STEPS:
        tx, ty, tc = plane_peer(i, x, y, c)
        pltpu.make_async_remote_copy(
            pieces.at[plane_index(tx, ty, tc), nine], r1.at[own, nine], sems.at[0], sems.at[1],
            device_id=device(tx, ty, z, tc), device_id_type=MESH,
        ).start()
    r1[own] = pieces[own]
    first()
    plane = r1.at[pl.ds(0, 31), nine]
    pltpu.make_async_copy(plane, plane, sems.at[1]).wait()
    tile, extra = r1[0, 0:8], r1[0, 8:9]
    for i in range(1, 32):
        tile = tile + r1[i, 0:8]
        extra = extra + r1[i, 8:9]
    part[0, 0:8] = tile
    part[0, 8:9] = extra
    for dz in Z_STEPS:
        pltpu.make_async_remote_copy(
            part.at[0, nine], r2.at[z, nine], sems.at[2], sems.at[3],
            device_id=device(x, y, (z + dz + 16) % 16, c), device_id_type=MESH,
        ).start()
    r2[z, 0:8] = tile
    r2[z, 8:9] = extra
    ring = r2.at[pl.ds(0, 15), nine]
    pltpu.make_async_copy(ring, ring, sems.at[3]).wait()
    tile, extra = r2[0, 0:8], r2[0, 8:9]
    for i in range(1, 16):
        tile = tile + r2[i, 0:8]
        extra = extra + r2[i, 8:9]
    part[1, 0:8] = tile
    for i in PLANE_STEPS:
        tx, ty, tc = plane_peer(i, x, y, c)
        pltpu.make_async_remote_copy(
            part.at[1, pl.ds(0, 8)], full.at[own], sems.at[4], sems.at[5],
            device_id=device(tx, ty, z, tc), device_id_type=MESH,
        ).start()
    full[own] = tile
    last()
    pltpu.make_async_copy(plane, plane, sems.at[0]).wait()
    pltpu.make_async_copy(ring, ring, sems.at[2]).wait()
    tiles = full.at[pl.ds(0, 31)]
    pltpu.make_async_copy(tiles, tiles, sems.at[5]).wait()
    b = full[0:16].reshape(128, 128)
    t = full[16:32].reshape(128, 128)
    turned = t.T
    gram[:128, :128] = jnp.where(row >= col, t, turned)
    gram[:128, 128:] = b
    gram[128:, :128] = b.T
    gram[128:, 128:] = jnp.where(row < col, t, jnp.where(row > col, turned, extra))
    pltpu.make_async_copy(tiles, tiles, sems.at[4]).wait()


def kernel(
    x_hbm, sx_hbm, sy_hbm, sz_hbm, core, fx, fy, fz,
    xt, starts, outgoing, by_z, staged, lines, matrix, fc, sc, q, d, at, turned, perm_x, perm_z, vt, halves, gram,
    pieces, r1, r2, part, full, ar_sems, z_recv, near_recv, staged_recv, in_sems, sems,
):
    x, y, z, c = position()
    own = plane_index(x, y, c)
    loads = []
    for half in range(2):
        for rows in range(2):
            block = (pl.ds(64 * rows, 64), slice(None), pl.ds(128 * half, 128))
            loads.append(
                pltpu.make_async_copy(x_hbm.at[block], xt.at[block], in_sems.at[half * 2 + rows])
            )
    for i, start in enumerate((sx_hbm, sy_hbm, sz_hbm)):
        loads.append(pltpu.make_async_copy(start, starts.at[i], in_sems.at[4 + i]))
    for load in loads:
        load.start()
    barrier = pltpu.get_barrier_semaphore()
    for i in PLANE_STEPS:
        tx, ty, tc = plane_peer(i, x, y, c)
        pl.semaphore_signal(barrier, 1, device_id=device(tx, ty, z, tc), device_id_type=MESH)
    for dz in Z_STEPS:
        for dc in range(2):
            pl.semaphore_signal(
                barrier, 1, device_id=device(x, y, (z + dz + 16) % 16, (c + dc) % 2), device_id_type=MESH
            )

    sub = lax.broadcasted_iota(jnp.int32, (8, 128), 0)
    lane = lax.broadcasted_iota(jnp.int32, (8, 128), 1)
    keep = (sub < 4) == (lane < 64)
    for half in range(2):
        loads[2 * half].wait()
        loads[2 * half + 1].wait()
        for s in range(16):
            t = xt[:, s, half * 128 : half * 128 + 128].T
            for zb in range(16):
                tile = t[zb * 8 : zb * 8 + 8, :]
                moved = pltpu.roll(pltpu.roll(tile, 4, 0), 64, 1)
                outgoing[s, half * 16 + zb] = jnp.where(keep, tile, moved)
    pl.semaphore_wait(barrier, 61)

    def distance(k):
        d = 8 - (k + 1) // 2
        return d if k % 2 else -d

    def send_far(k):
        tz = (z + distance(k) + 16) % 16
        pltpu.make_async_remote_copy(
            outgoing.at[tz], by_z.at[z], sems.at[0], z_recv.at[k],
            device_id=device(x, y, tz, c), device_id_type=MESH,
        ).start()

    yc = y * 2 + c
    for k in range(3):
        send_far(k)
    for j, dz in enumerate(NEAR):
        tz = (z + dz + 16) % 16
        for i in PLANE_STEPS:
            tx, ty, tc = plane_peer(i, x, y, c)
            pltpu.make_async_remote_copy(
                outgoing.at[tz, plane_index(tx, ty, tc)], staged.at[j, x, yc],
                sems.at[1], staged_recv.at[j],
                device_id=device(tx, ty, z, tc), device_id_type=MESH,
            ).start()
        staged[j, x, yc] = outgoing[tz, own]
    for k in range(3, ROUNDS):
        send_far(k)

    def forward(buffer, slot):
        for i in PLANE_STEPS:
            tx, ty, tc = plane_peer(i, x, y, c)
            pltpu.make_async_remote_copy(
                buffer.at[slot, plane_index(tx, ty, tc)], lines.at[x, slot * 8 + yc],
                sems.at[1], sems.at[2],
                device_id=device(tx, ty, z, tc), device_id_type=MESH,
            ).start()
        lines[x, slot * 8 + yc] = buffer[slot, own]

    def forward_far(k, carry):
        block = by_z.at[0]
        pltpu.make_async_copy(block, block, z_recv.at[k]).wait()
        d = 8 - (k + 1) // 2
        forward(by_z, (z - d * (2 * (k % 2) - 1) + 16) % 16)
        return carry

    forward(outgoing, z)
    for load in loads[4:]:
        load.wait()
    perm_x[...] = permutation("x")
    perm_z[...] = permutation("z")
    vt[0] = dot(starts[0], perm_x[...], 1, 0)
    vt[1] = dot(starts[2], perm_z[...], 1, 0)

    lax.fori_loop(0, NEAR_AFTER, forward_far, 0)
    for j, dz in enumerate(NEAR):
        tiles = outgoing.at[0, pl.ds(0, 31)]
        pltpu.make_async_copy(tiles, tiles, staged_recv.at[j]).wait()
        tz = (z + dz + 16) % 16
        pltpu.make_async_remote_copy(
            staged.at[j], lines.at[:, pl.ds(z * 8, 8)], sems.at[7], near_recv.at[j],
            device_id=device(x, y, tz, c), device_id_type=MESH,
        ).start()
    lax.fori_loop(NEAR_AFTER, ROUNDS, forward_far, 0)
    tiles = outgoing.at[pl.ds(0, ROUNDS + 1), pl.ds(0, 31)]
    pltpu.make_async_copy(tiles, tiles, sems.at[2]).wait()
    for j in range(len(NEAR)):
        block = staged.at[j]
        pltpu.make_async_copy(block, block, near_recv.at[j]).wait()

    for cx in range(4):
        for zh in range(4):
            for p in range(2):
                matrix[p * 128 : p * 128 + 128, (cx * 4 + zh) * 128 : (cx * 4 + zh + 1) * 128] = (
                    lines[cx, :, p * 4 + zh, :]
                )
    def reduce_gram(k, g, first=nothing, last=nothing):
        all_reduce(
            g, gram, pieces.at[k], r1.at[k], r2.at[k], part.at[k], full.at[k], ar_sems.at[k], first, last
        )

    def sent():
        far = outgoing.at[pl.ds(0, ROUNDS)]
        pltpu.make_async_copy(far, far, sems.at[0]).wait()
        tiles = outgoing.at[:, pl.ds(0, 31)]
        pltpu.make_async_copy(tiles, tiles, sems.at[1]).wait()
        pltpu.make_async_copy(staged, staged, sems.at[7]).wait()

    reduce_gram(0, dot(matrix[...], matrix[...], 1, 1), first=sent)
    vt[2] = factor(gram, vt[0])

    low = lax.broadcasted_iota(jnp.int32, (64, 128), 1) < 64
    for zh in range(4):
        piece = [
            dot(vt[2], matrix[:, (cx * 4 + zh) * 128 : (cx * 4 + zh + 1) * 128], 1, 0)
            for cx in range(4)
        ]
        shifted = [pltpu.roll(v, 64, 1) for v in piece]
        for pair in range(2):
            a, b = 2 * pair, 2 * pair + 1
            for zl, value in (
                (0, jnp.where(low, piece[a], shifted[b])),
                (1, jnp.where(low, shifted[a], piece[b])),
            ):
                zz = zl * 4 + zh
                for kb in range(4):
                    fc[kb * 128 + zz * 16 : kb * 128 + zz * 16 + 16, pair * 128 : pair * 128 + 128] = (
                        value[kb * 16 : kb * 16 + 16, :]
                    )
    def finish_x():
        fx[...] = dot(vt[2], perm_x[...], 1, 1)

    reduce_gram(1, dot(fc[...], fc[...], 0, 0), first=finish_x)
    fy[...] = factor(gram, starts[1])

    for lanes in range(2):
        halves[lanes] = fy[:, lanes * 128 : lanes * 128 + 128]
        for cy in range(4):
            for half in range(2):
                first = (cy * 2 + half) * 8
                vt[2, first : first + 8, lanes * 128 : lanes * 128 + 128] = halves[
                    lanes, pl.ds(32 * half + cy, 8, stride=4), :
                ]
    product = dot(vt[2], fc[...], 1, 1)
    for t in range(8):
        for cx in range(4):
            sc[t * 4 + cx] = product[t * 8 : t * 8 + 8, cx * 128 : cx * 128 + 128]

    for i in range(1, 32):
        tx, ty, tc = plane_peer(i, x, y, c)
        pltpu.make_async_remote_copy(
            sc.at[plane_index(tx, ty, tc)], q.at[own], sems.at[3], sems.at[4],
            device_id=device(tx, ty, z, tc), device_id_type=MESH,
        ).start()
    q[own] = sc[own]
    tiles = sc.at[pl.ds(0, 31)]
    pltpu.make_async_copy(tiles, tiles, sems.at[4]).wait()
    pltpu.make_async_copy(tiles, tiles, sems.at[3]).wait()

    for m in range(8):
        at[1, m * 32 : m * 32 + 32, :] = q[:, m, :]
    lines_z = swap_blocks([at[1, m * 32 : m * 32 + 32, :] for m in range(8)])
    for zz in range(8):
        at[0, zz * 32 : zz * 32 + 32, :] = lines_z[zz]
    tc = z // 8

    def send_lines():
        for m in range(8):
            tz = c * 8 + m

            @pl.when(jnp.logical_or(tz != z, tc != c))
            def _():
                pltpu.make_async_remote_copy(
                    at.at[1, pl.ds(m * 32, 32), :], d.at[z % 8], sems.at[5], sems.at[6],
                    device_id=device(x, y, tz, tc), device_id_type=MESH,
                ).start()

            @pl.when(jnp.logical_and(tz == z, tc == c))
            def _():
                d[z % 8] = at[1, m * 32 : m * 32 + 32, :]

    def take_lines():
        @pl.when(tc == c)
        def _():
            seven = d.at[pl.ds(0, 7)]
            pltpu.make_async_copy(seven, seven, sems.at[6]).wait()
            pltpu.make_async_copy(seven, seven, sems.at[5]).wait()

        @pl.when(tc != c)
        def _():
            pltpu.make_async_copy(d, d, sems.at[6]).wait()
            pltpu.make_async_copy(d, d, sems.at[5]).wait()

        by_zz = swap_blocks([d[s] for s in range(8)])
        for zz in range(8):
            at[0, zz * 32 : zz * 32 + 32, :] = by_zz[zz]
        for half in range(2):
            turned[:, half * 128 : half * 128 + 128] = at[0, half * 128 : half * 128 + 128, :].T

    reduce_gram(2, dot(at[0], at[0], 1, 1), first=send_lines, last=take_lines)
    vt[2] = factor(gram, vt[1])
    result = dot(turned[...], vt[2], 1, 1)
    for s in range(8):
        core[s] = result[s * 16 : s * 16 + 16, :]
    fz[...] = dot(vt[2], perm_z[...], 1, 1)


def write_out(*refs):
    sources, targets, sems = refs[:4], refs[4:8], refs[8]
    copies = [pltpu.make_async_copy(a, b, sems.at[i]) for i, (a, b) in enumerate(zip(sources, targets))]
    for copy in copies:
        copy.start()
    for copy in copies:
        copy.wait()


def local(x_data, start_x, start_y, start_z):
    f32 = jnp.float32
    vmem = pl.BlockSpec(memory_space=pltpu.VMEM)
    hbm = pl.BlockSpec(memory_space=pltpu.HBM)
    xt = jnp.transpose(x_data, (0, 2, 3, 1)).reshape(128, 16, 256)
    shapes = [
        jax.ShapeDtypeStruct((8, 16, 64), f32),
        jax.ShapeDtypeStruct((64, 256), f32),
        jax.ShapeDtypeStruct((64, 256), f32),
        jax.ShapeDtypeStruct((64, 256), f32),
    ]
    results = pl.pallas_call(
        kernel,
        out_shape=shapes,
        in_specs=[hbm] * 4,
        out_specs=[vmem] * 4,
        scratch_shapes=[
            pltpu.VMEM((128, 16, 256), f32),
            pltpu.VMEM((3, 64, 256), f32),
            pltpu.VMEM((16, 32, 8, 128), f32),
            pltpu.VMEM((16, 32, 8, 128), f32),
            pltpu.VMEM((4, 4, 8, 8, 128), f32),
            pltpu.VMEM((4, 128, 8, 128), f32),
            pltpu.VMEM((256, 2048), f32),
            pltpu.VMEM((512, 256), f32),
            pltpu.VMEM((32, 8, 128), f32),
            pltpu.VMEM((32, 8, 128), f32),
            pltpu.VMEM((8, 32, 128), f32),
            pltpu.VMEM((2, 256, 128), f32),
            pltpu.VMEM((128, 256), f32),
            pltpu.VMEM((256, 256), f32),
            pltpu.VMEM((256, 256), f32),
            pltpu.VMEM((3, 64, 256), f32),
            pltpu.VMEM((2, 64, 128), f32),
            pltpu.VMEM((256, 256), f32),
            pltpu.VMEM((3, 32, 16, 128), f32),
            pltpu.VMEM((3, 32, 16, 128), f32),
            pltpu.VMEM((3, 16, 16, 128), f32),
            pltpu.VMEM((3, 2, 16, 128), f32),
            pltpu.VMEM((3, 32, 8, 128), f32),
            pltpu.SemaphoreType.DMA((3, 6)),
            pltpu.SemaphoreType.DMA((ROUNDS,)),
            pltpu.SemaphoreType.DMA((len(NEAR),)),
            pltpu.SemaphoreType.DMA((len(NEAR),)),
            pltpu.SemaphoreType.DMA((7,)),
            pltpu.SemaphoreType.DMA((8,)),
        ],
        compiler_params=pltpu.CompilerParams(
            collective_id=0, has_side_effects=True, vmem_limit_bytes=63 << 20
        ),
    )(xt, start_x.T, start_y.T, start_z.T)
    core, fx, fy, fz = pl.pallas_call(
        write_out,
        out_shape=shapes,
        in_specs=[hbm] * 4,
        out_specs=[hbm] * 4,
        scratch_shapes=[pltpu.SemaphoreType.DMA((4,))],
    )(*results)
    return core, fx.T, fy.T, fz.T


def solution(mesh):
    placed = (P("gx", None, "gy", None), P(), P(), P())
    return jax.shard_map(
        local,
        mesh=mesh,
        in_specs=placed,
        out_specs=(P("gx", "gy", None), P(), P(), P()),
        check_vma=False,
    )
```

```python
import functools

import jax
import jax.numpy as jnp
from jax import lax
from jax.experimental import pallas as pl
from jax.experimental.pallas import tpu as pltpu
from jax.sharding import PartitionSpec as P

ITERS = 4
MESH = pl.DeviceIdType.MESH
HIGHEST = lax.Precision.HIGHEST
ROUNDS = 11
NEAR = (2, -2, 1, -1)
NEAR_AFTER = 8
Z_STEPS = [8] + [sign * d for d in range(7, 0, -1) for sign in (1, -1)]


def plane_distance(i):
    dx, dy, dc = i % 4, i // 8, (i // 4) % 2
    return min(dx, 4 - dx) + min(dy, 4 - dy) + dc


PLANE_STEPS = sorted(range(1, 32), key=lambda i: -plane_distance(i))


def dot(a, b, ca, cb):
    return lax.dot_general(
        a, b, (((ca,), (cb,)), ((), ())), precision=HIGHEST, preferred_element_type=jnp.float32
    )


def position():
    g = lax.axis_index("gx")
    return lax.axis_index("gy"), (g // 2) % 4, g // 8, g % 2


def device(x, y, z, c):
    return ((z * 4 + y) * 2 + c, x)


def plane_index(x, y, c):
    return (y * 2 + c) * 4 + x


def plane_peer(i, x, y, c):
    return (x + i % 4) % 4, (y + i // 8) % 4, (c + (i // 4) % 2) % 2


def inverse_cholesky(p):
    n = 64
    row = lax.broadcasted_iota(jnp.int32, (n, n), 0)
    col = lax.broadcasted_iota(jnp.int32, (n, n), 1)
    m = jnp.concatenate([p, (row == col).astype(jnp.float32)], axis=1)
    sub = lax.broadcasted_iota(jnp.int32, (8, 128), 0)
    blocks = [m[8 * i : 8 * i + 8, :] for i in range(8)]
    out = []
    for k in range(8):
        cols = {
            (i, j): jnp.broadcast_to(blocks[i][:, 8 * k + j : 8 * k + j + 1], (8, 128))
            for j in range(8)
            for i in range(k, 8)
        }
        rows = [jnp.broadcast_to(blocks[k][j : j + 1, :], (8, 128)) for j in range(8)]
        for j in range(8):
            scale = lax.rsqrt(jnp.broadcast_to(cols[k, j][j : j + 1, :], (8, 128)))
            for i in range(k, 8):
                cols[i, j] = cols[i, j] * scale
            rows[j] = rows[j] * scale
            for t in range(j + 1, 8):
                factor_t = jnp.broadcast_to(cols[k, j][t : t + 1, :], (8, 128))
                for i in range(k, 8):
                    cols[i, t] = cols[i, t] - cols[i, j] * factor_t
                rows[t] = rows[t] - rows[j] * factor_t
        for i in range(k + 1, 8):
            for j in range(8):
                blocks[i] = blocks[i] - cols[i, j] * rows[j]
        done = rows[0]
        for j in range(1, 8):
            done = jnp.where(sub == j, rows[j], done)
        out.append(done)
    return jnp.concatenate(out, axis=0)[:, n:]


def factor(gram, start_t):
    def step(_, block):
        image = dot(block, gram[...], 1, 0)
        return dot(inverse_cholesky(dot(image, image, 1, 1)), image, 1, 0)

    return lax.fori_loop(0, ITERS, step, start_t)


def permutation(kind):
    old = lax.broadcasted_iota(jnp.int32, (256, 256), 0)
    new = lax.broadcasted_iota(jnp.int32, (256, 256), 1)
    if kind == "x":
        source = (new % 128) * 2 + new // 128
    else:
        source = (new % 32) * 8 + new // 32
    return (old == source).astype(jnp.float32)


def swap_blocks(parts):
    lane = lax.broadcasted_iota(jnp.int32, (32, 128), 1) // 16
    parts = list(parts)
    for bit in (1, 2, 4):
        high = (lane & bit) != 0
        new = list(parts)
        for a in range(8):
            if a & bit == 0:
                lo, hi = parts[a], parts[a + bit]
                new[a] = jnp.where(high, pltpu.roll(hi, 16 * bit, 1), lo)
                new[a + bit] = jnp.where(high, hi, pltpu.roll(lo, 128 - 16 * bit, 1))
        parts = new
    return parts


def nothing():
    pass


def all_reduce(g, gram, pieces, r1, r2, part, full, sems, first=nothing, last=nothing):
    x, y, z, c = position()
    own = plane_index(x, y, c)
    row = lax.broadcasted_iota(jnp.int32, (128, 128), 0)
    col = lax.broadcasted_iota(jnp.int32, (128, 128), 1)
    low_right = g[128:, 128:]
    diagonal = jnp.sum(jnp.where(row == col, low_right, 0.0), axis=0, keepdims=True)
    t = jnp.where(row >= col, g[:128, :128], low_right)
    b = g[:128, 128:]
    beside = jnp.broadcast_to(diagonal, (8, 128))
    for q in range(16):
        pieces[q, 0:8] = b[8 * q : 8 * q + 8, :]
        pieces[16 + q, 0:8] = t[8 * q : 8 * q + 8, :]
        pieces[q, 8:16] = beside
        pieces[16 + q, 8:16] = beside
    nine = pl.ds(0, 9)
    for i in PLANE_STEPS:
        tx, ty, tc = plane_peer(i, x, y, c)
        pltpu.make_async_remote_copy(
            pieces.at[plane_index(tx, ty, tc), nine], r1.at[own, nine], sems.at[0], sems.at[1],
            device_id=device(tx, ty, z, tc), device_id_type=MESH,
        ).start()
    r1[own] = pieces[own]
    first()
    plane = r1.at[pl.ds(0, 31), nine]
    pltpu.make_async_copy(plane, plane, sems.at[1]).wait()
    tile, extra = r1[0, 0:8], r1[0, 8:9]
    for i in range(1, 32):
        tile = tile + r1[i, 0:8]
        extra = extra + r1[i, 8:9]
    part[0, 0:8] = tile
    part[0, 8:9] = extra
    for dz in Z_STEPS:
        pltpu.make_async_remote_copy(
            part.at[0, nine], r2.at[z, nine], sems.at[2], sems.at[3],
            device_id=device(x, y, (z + dz + 16) % 16, c), device_id_type=MESH,
        ).start()
    r2[z, 0:8] = tile
    r2[z, 8:9] = extra
    ring = r2.at[pl.ds(0, 15), nine]
    pltpu.make_async_copy(ring, ring, sems.at[3]).wait()
    tile, extra = r2[0, 0:8], r2[0, 8:9]
    for i in range(1, 16):
        tile = tile + r2[i, 0:8]
        extra = extra + r2[i, 8:9]
    part[1, 0:8] = tile
    for i in PLANE_STEPS:
        tx, ty, tc = plane_peer(i, x, y, c)
        pltpu.make_async_remote_copy(
            part.at[1, pl.ds(0, 8)], full.at[own], sems.at[4], sems.at[5],
            device_id=device(tx, ty, z, tc), device_id_type=MESH,
        ).start()
    full[own] = tile
    last()
    pltpu.make_async_copy(plane, plane, sems.at[0]).wait()
    pltpu.make_async_copy(ring, ring, sems.at[2]).wait()
    tiles = full.at[pl.ds(0, 31)]
    pltpu.make_async_copy(tiles, tiles, sems.at[5]).wait()
    b = full[0:16].reshape(128, 128)
    t = full[16:32].reshape(128, 128)
    turned = t.T
    gram[:128, :128] = jnp.where(row >= col, t, turned)
    gram[:128, 128:] = b
    gram[128:, :128] = b.T
    gram[128:, 128:] = jnp.where(row < col, t, jnp.where(row > col, turned, extra))
    pltpu.make_async_copy(tiles, tiles, sems.at[4]).wait()


def kernel(
    x_hbm, sx_hbm, sy_hbm, sz_hbm, core, fx, fy, fz,
    xt, starts, outgoing, by_z, staged, lines, matrix, fc, sc, q, d, at, turned, perm_x, perm_z, vt, halves, gram,
    pieces, r1, r2, part, full, ar_sems, z_recv, near_recv, staged_recv, in_sems, sems,
):
    x, y, z, c = position()
    own = plane_index(x, y, c)
    loads = []
    for half in range(2):
        for rows in range(2):
            some = pl.ds(64 * rows, 64)
            loads.append(
                pltpu.make_async_copy(
                    x_hbm.at[some, :, pl.ds(128 * half, 128)], xt.at[half, some], in_sems.at[half * 2 + rows]
                )
            )
    for i, start in enumerate((sx_hbm, sy_hbm, sz_hbm)):
        loads.append(pltpu.make_async_copy(start, starts.at[i], in_sems.at[4 + i]))
    for load in loads:
        load.start()
    barrier = pltpu.get_barrier_semaphore()
    for i in PLANE_STEPS:
        tx, ty, tc = plane_peer(i, x, y, c)
        pl.semaphore_signal(barrier, 1, device_id=device(tx, ty, z, tc), device_id_type=MESH)
    for dz in Z_STEPS:
        for dc in range(2):
            pl.semaphore_signal(
                barrier, 1, device_id=device(x, y, (z + dz + 16) % 16, (c + dc) % 2), device_id_type=MESH
            )

    sub = lax.broadcasted_iota(jnp.int32, (8, 128), 0)
    lane = lax.broadcasted_iota(jnp.int32, (8, 128), 1)
    keep = (sub < 4) == (lane < 64)
    by_row = xt.reshape(2, 2048, 128)
    for half in range(2):
        loads[2 * half].wait()
        loads[2 * half + 1].wait()
        for s in range(16):
            t = by_row[half, pl.ds(s, 128, stride=16), :].T
            for zb in range(16):
                tile = t[zb * 8 : zb * 8 + 8, :]
                moved = pltpu.roll(pltpu.roll(tile, 4, 0), 64, 1)
                outgoing[s, half * 16 + zb] = jnp.where(keep, tile, moved)
    pl.semaphore_wait(barrier, 61)

    def distance(k):
        d = 8 - (k + 1) // 2
        return d if k % 2 else -d

    def send_far(k):
        tz = (z + distance(k) + 16) % 16
        pltpu.make_async_remote_copy(
            outgoing.at[tz], by_z.at[z], sems.at[0], z_recv.at[k],
            device_id=device(x, y, tz, c), device_id_type=MESH,
        ).start()

    yc = y * 2 + c
    for k in range(3):
        send_far(k)
    for j, dz in enumerate(NEAR):
        tz = (z + dz + 16) % 16
        for i in PLANE_STEPS:
            tx, ty, tc = plane_peer(i, x, y, c)
            pltpu.make_async_remote_copy(
                outgoing.at[tz, plane_index(tx, ty, tc)], staged.at[j, x, yc],
                sems.at[1], staged_recv.at[j],
                device_id=device(tx, ty, z, tc), device_id_type=MESH,
            ).start()
        staged[j, x, yc] = outgoing[tz, own]
    for k in range(3, ROUNDS):
        send_far(k)

    def forward(buffer, slot):
        for i in PLANE_STEPS:
            tx, ty, tc = plane_peer(i, x, y, c)
            pltpu.make_async_remote_copy(
                buffer.at[slot, plane_index(tx, ty, tc)], lines.at[x, slot * 8 + yc],
                sems.at[1], sems.at[2],
                device_id=device(tx, ty, z, tc), device_id_type=MESH,
            ).start()
        lines[x, slot * 8 + yc] = buffer[slot, own]

    def forward_far(k, carry):
        block = by_z.at[0]
        pltpu.make_async_copy(block, block, z_recv.at[k]).wait()
        d = 8 - (k + 1) // 2
        forward(by_z, (z - d * (2 * (k % 2) - 1) + 16) % 16)
        return carry

    forward(outgoing, z)
    for load in loads[4:]:
        load.wait()
    perm_x[...] = permutation("x")
    perm_z[...] = permutation("z")
    vt[0] = dot(starts[0], perm_x[...], 1, 0)
    vt[1] = dot(starts[2], perm_z[...], 1, 0)

    lax.fori_loop(0, NEAR_AFTER, forward_far, 0)
    for j, dz in enumerate(NEAR):
        tiles = outgoing.at[0, pl.ds(0, 31)]
        pltpu.make_async_copy(tiles, tiles, staged_recv.at[j]).wait()
        tz = (z + dz + 16) % 16
        pltpu.make_async_remote_copy(
            staged.at[j], lines.at[:, pl.ds(z * 8, 8)], sems.at[7], near_recv.at[j],
            device_id=device(x, y, tz, c), device_id_type=MESH,
        ).start()
    lax.fori_loop(NEAR_AFTER, ROUNDS, forward_far, 0)
    tiles = outgoing.at[pl.ds(0, ROUNDS + 1), pl.ds(0, 31)]
    pltpu.make_async_copy(tiles, tiles, sems.at[2]).wait()
    for j in range(len(NEAR)):
        block = staged.at[j]
        pltpu.make_async_copy(block, block, near_recv.at[j]).wait()

    line_rows = lines.reshape(4, 1024, 128)
    for cx in range(4):
        for zh in range(4):
            for p in range(2):
                matrix[p * 128 : p * 128 + 128, (cx * 4 + zh) * 128 : (cx * 4 + zh + 1) * 128] = (
                    line_rows[cx, pl.ds(p * 4 + zh, 128, stride=8), :]
                )
    def reduce_gram(k, g, first=nothing, last=nothing):
        all_reduce(
            g, gram, pieces.at[k], r1.at[k], r2.at[k], part.at[k], full.at[k], ar_sems.at[k], first, last
        )

    def sent():
        far = outgoing.at[pl.ds(0, ROUNDS)]
        pltpu.make_async_copy(far, far, sems.at[0]).wait()
        tiles = outgoing.at[:, pl.ds(0, 31)]
        pltpu.make_async_copy(tiles, tiles, sems.at[1]).wait()
        pltpu.make_async_copy(staged, staged, sems.at[7]).wait()

    reduce_gram(0, dot(matrix[...], matrix[...], 1, 1), first=sent)
    vt[2] = factor(gram, vt[0])

    low = lax.broadcasted_iota(jnp.int32, (64, 128), 1) < 64
    for zh in range(4):
        piece = [
            dot(vt[2], matrix[:, (cx * 4 + zh) * 128 : (cx * 4 + zh + 1) * 128], 1, 0)
            for cx in range(4)
        ]
        shifted = [pltpu.roll(v, 64, 1) for v in piece]
        for pair in range(2):
            a, b = 2 * pair, 2 * pair + 1
            for zl, value in (
                (0, jnp.where(low, piece[a], shifted[b])),
                (1, jnp.where(low, shifted[a], piece[b])),
            ):
                zz = zl * 4 + zh
                for kb in range(4):
                    fc[kb * 128 + zz * 16 : kb * 128 + zz * 16 + 16, pair * 128 : pair * 128 + 128] = (
                        value[kb * 16 : kb * 16 + 16, :]
                    )
    def finish_x():
        fx[...] = dot(vt[2], perm_x[...], 1, 1)

    reduce_gram(1, dot(fc[...], fc[...], 0, 0), first=finish_x)
    fy[...] = factor(gram, starts[1])

    for lanes in range(2):
        halves[lanes] = fy[:, lanes * 128 : lanes * 128 + 128]
        for cy in range(4):
            for half in range(2):
                first = (cy * 2 + half) * 8
                vt[2, first : first + 8, lanes * 128 : lanes * 128 + 128] = halves[
                    lanes, pl.ds(32 * half + cy, 8, stride=4), :
                ]
    product = dot(vt[2], fc[...], 1, 1)
    for t in range(8):
        for cx in range(4):
            sc[t * 4 + cx] = product[t * 8 : t * 8 + 8, cx * 128 : cx * 128 + 128]

    for i in range(1, 32):
        tx, ty, tc = plane_peer(i, x, y, c)
        pltpu.make_async_remote_copy(
            sc.at[plane_index(tx, ty, tc)], q.at[own], sems.at[3], sems.at[4],
            device_id=device(tx, ty, z, tc), device_id_type=MESH,
        ).start()
    q[own] = sc[own]
    tiles = sc.at[pl.ds(0, 31)]
    pltpu.make_async_copy(tiles, tiles, sems.at[4]).wait()
    pltpu.make_async_copy(tiles, tiles, sems.at[3]).wait()

    for m in range(8):
        at[1, m * 32 : m * 32 + 32, :] = q.reshape(256, 128)[pl.ds(m, 32, stride=8), :]
    lines_z = swap_blocks([at[1, m * 32 : m * 32 + 32, :] for m in range(8)])
    for zz in range(8):
        at[0, zz * 32 : zz * 32 + 32, :] = lines_z[zz]
    tc = z // 8

    def send_lines():
        for m in range(8):
            tz = c * 8 + m

            @pl.when(jnp.logical_or(tz != z, tc != c))
            def _():
                pltpu.make_async_remote_copy(
                    at.at[1, pl.ds(m * 32, 32), :], d.at[z % 8], sems.at[5], sems.at[6],
                    device_id=device(x, y, tz, tc), device_id_type=MESH,
                ).start()

            @pl.when(jnp.logical_and(tz == z, tc == c))
            def _():
                d[z % 8] = at[1, m * 32 : m * 32 + 32, :]

    def take_lines():
        @pl.when(tc == c)
        def _():
            seven = d.at[pl.ds(0, 7)]
            pltpu.make_async_copy(seven, seven, sems.at[6]).wait()
            pltpu.make_async_copy(seven, seven, sems.at[5]).wait()

        @pl.when(tc != c)
        def _():
            pltpu.make_async_copy(d, d, sems.at[6]).wait()
            pltpu.make_async_copy(d, d, sems.at[5]).wait()

        by_zz = swap_blocks([d[s] for s in range(8)])
        for zz in range(8):
            at[0, zz * 32 : zz * 32 + 32, :] = by_zz[zz]
        for half in range(2):
            turned[:, half * 128 : half * 128 + 128] = at[0, half * 128 : half * 128 + 128, :].T

    reduce_gram(2, dot(at[0], at[0], 1, 1), first=send_lines, last=take_lines)
    vt[2] = factor(gram, vt[1])
    result = dot(turned[...], vt[2], 1, 1)
    for s in range(8):
        core[s] = result[s * 16 : s * 16 + 16, :]
    fz[...] = dot(vt[2], perm_z[...], 1, 1)


def write_out(*refs):
    sources, targets, held, sems = refs[:4], refs[4:8], refs[8:12], refs[12]
    into = [pltpu.make_async_copy(sources[i], held[i], sems.at[i]) for i in range(4)]
    out = [pltpu.make_async_copy(held[i], targets[i], sems.at[4 + i]) for i in range(4)]
    for copy in into:
        copy.start()
    for i in range(4):
        into[i].wait()
        out[i].start()
    for copy in out:
        copy.wait()


def local(x_data, start_x, start_y, start_z):
    f32 = jnp.float32
    vmem = pl.BlockSpec(memory_space=pltpu.VMEM)
    hbm = pl.BlockSpec(memory_space=pltpu.HBM)
    xt = jnp.transpose(x_data, (0, 2, 3, 1)).reshape(128, 16, 256)
    shapes = [
        jax.ShapeDtypeStruct((8, 16, 64), f32),
        jax.ShapeDtypeStruct((64, 256), f32),
        jax.ShapeDtypeStruct((64, 256), f32),
        jax.ShapeDtypeStruct((64, 256), f32),
    ]
    results = pl.pallas_call(
        kernel,
        out_shape=shapes,
        in_specs=[hbm] * 4,
        out_specs=[vmem] * 4,
        scratch_shapes=[
            pltpu.VMEM((2, 128, 16, 128), f32),
            pltpu.VMEM((3, 64, 256), f32),
            pltpu.VMEM((16, 32, 8, 128), f32),
            pltpu.VMEM((16, 32, 8, 128), f32),
            pltpu.VMEM((4, 4, 8, 8, 128), f32),
            pltpu.VMEM((4, 128, 8, 128), f32),
            pltpu.VMEM((256, 2048), f32),
            pltpu.VMEM((512, 256), f32),
            pltpu.VMEM((32, 8, 128), f32),
            pltpu.VMEM((32, 8, 128), f32),
            pltpu.VMEM((8, 32, 128), f32),
            pltpu.VMEM((2, 256, 128), f32),
            pltpu.VMEM((128, 256), f32),
            pltpu.VMEM((256, 256), f32),
            pltpu.VMEM((256, 256), f32),
            pltpu.VMEM((3, 64, 256), f32),
            pltpu.VMEM((2, 64, 128), f32),
            pltpu.VMEM((256, 256), f32),
            pltpu.VMEM((3, 32, 16, 128), f32),
            pltpu.VMEM((3, 32, 16, 128), f32),
            pltpu.VMEM((3, 16, 16, 128), f32),
            pltpu.VMEM((3, 2, 16, 128), f32),
            pltpu.VMEM((3, 32, 8, 128), f32),
            pltpu.SemaphoreType.DMA((3, 6)),
            pltpu.SemaphoreType.DMA((ROUNDS,)),
            pltpu.SemaphoreType.DMA((len(NEAR),)),
            pltpu.SemaphoreType.DMA((len(NEAR),)),
            pltpu.SemaphoreType.DMA((7,)),
            pltpu.SemaphoreType.DMA((8,)),
        ],
        compiler_params=pltpu.CompilerParams(
            collective_id=0, has_side_effects=True, vmem_limit_bytes=63 << 20
        ),
    )(xt, start_x.T, start_y.T, start_z.T)
    core, fx, fy, fz = pl.pallas_call(
        write_out,
        out_shape=shapes,
        in_specs=[hbm] * 4,
        out_specs=[hbm] * 4,
        scratch_shapes=[pltpu.VMEM(shape.shape, f32) for shape in shapes] + [pltpu.SemaphoreType.DMA((8,))],
        compiler_params=pltpu.CompilerParams(vmem_limit_bytes=63 << 20),
    )(*results)
    return core, fx.T, fy.T, fz.T


def solution(mesh):
    placed = (P("gx", None, "gy", None), P(), P(), P())
    return jax.shard_map(
        local,
        mesh=mesh,
        in_specs=placed,
        out_specs=(P("gx", "gy", None), P(), P(), P()),
        check_vma=False,
    )
```
